256 devices in a mesh: row: 4 (over x_hi, core), col: 64 (over z, y, x_lo).
Axes of the slice: x: 4 (x_hi: 2, x_lo: 2; x = x_hi * 2 + x_lo), y: 4, z: 8, core: 2. Of those that a mesh axis runs over, the one named last changes fastest.
Arguments:
- green_vectors: float32 [512, 131072], P('row', 'col'), may hold values from -6 to 6
- amplitudes: float32 [2048, 131072], P('row', 'col'), may hold values from -0.015625 to 0.015625
- cholesky: float32 [2048, 4096], P(('row', 'col')), may hold values from -0.125 to 0.125
Outputs:
- force_bias: float32 [512, 4096], P('col', 'row')
The draws below stay inside these ranges and needn't reach their ends.
All inputs are finite; a program needn't handle non-finite values.
Results may differ from the reference program's by a relative error of at most 0.000084.
Values sent between devices are 32-bit elements; how exact they have to be, the bound alone decides.
No kernel may reach another device: no remote copies, remote signals or barrier semaphores. Data moves between devices by JAX's collectives and lax.ppermute only.
A program may use at most 64 MiB of HBM per device.

```python
import jax
import jax.numpy as jnp
from jax import lax

NCHOL = 4096
WALKERS = 512
PAIRS = 131072
SLAB = 2048


def level_of(rng, shape, shards, low, largest):
    def one(position, parts):
        heights = jax.random.uniform(jax.random.fold_in(jax.random.fold_in(rng, 6), position), (parts,), jnp.float32, low / len(shards), largest / len(shards))
        return jnp.repeat(jnp.exp(heights), shape[position] // parts).reshape((-1,) + (1,) * (len(shape) - position - 1))

    factor_of = one(*shards[0])
    for cut in shards[1:]:
        factor_of = factor_of * one(*cut)
    return factor_of


def noise(rng, dims, width, bound, shards=(), dtype=jnp.bfloat16):
    result = width * jax.random.normal(rng, dims, jnp.float32)
    if shards:
        result = result * level_of(rng, dims, shards, -0.22, 0.18)
    return jnp.clip(result, -bound, bound).astype(dtype)


def setup_inputs(seed: int = 0) -> dict:
    arg_keys = jax.random.split(jax.random.key(seed), 4)
    green_vectors = noise(arg_keys[0], (WALKERS, PAIRS), 1.0, 6.0, ((0, 4), (1, 64)), jnp.float32)
    amplitudes = noise(arg_keys[1], (SLAB, PAIRS), PAIRS ** -0.5, 0.015625, ((0, 4), (1, 64)), jnp.float32)
    cholesky = noise(arg_keys[2], (SLAB, NCHOL), SLAB ** -0.5, 0.125, ((0, 256),), jnp.float32)
    return dict(green_vectors=green_vectors, amplitudes=amplitudes, cholesky=cholesky)


def reference(green_vectors, amplitudes, cholesky):
    effective = lax.dot_general(green_vectors, amplitudes, (((1,), (1,)), ((), ())), precision=lax.Precision.HIGHEST, preferred_element_type=jnp.float32)
    return jnp.dot(effective, cholesky, precision=lax.Precision.HIGHEST, preferred_element_type=jnp.float32)
```

```python
import itertools

import jax
import jax.numpy as jnp
import numpy as np
from jax import lax
from jax.sharding import Mesh, PartitionSpec as P

SIZES = {"xh": 2, "c": 2, "zh": 4, "z0": 2, "yh": 2, "y0": 2, "xl": 2}
AXES = tuple(SIZES)
ROW = ("xh", "c")
COL = ("zh", "z0", "yh", "y0", "xl")
HIGH = lax.Precision.HIGH


def move(x, axis):
    return lax.ppermute(x, axis, [(0, 1), (1, 0)])


def exchange(pieces, axes):
    got = lax.all_to_all(pieces, axes, 0, 0, tiled=True)
    return jnp.sum(got, axis=0)


def partial_terms(green, amplitudes):
    walkers = green.reshape(256, -1)
    terms = lax.dot_general(
        walkers, amplitudes, (((1,), (1,)), ((), ())), precision=HIGH, preferred_element_type=jnp.float32
    )
    terms = terms.reshape(2, 4, 32, 4, 128).transpose(1, 3, 0, 2, 4).reshape(16, 64, 128)
    return exchange(terms, ("z0", "yh", "y0", "xl")).reshape(2, 32, 128)


def per_device(green, amplitudes, cholesky):
    green_x = move(green, "xh")
    green_c = move(green, "c")
    factors = lax.all_gather(cholesky, ("zh", "z0", "yh"), axis=0, tiled=True)

    amplitudes = amplitudes.reshape(16, 4, 8, -1).transpose(1, 0, 2, 3).reshape(512, -1)
    near = partial_terms(jnp.stack([green, green_c]), amplitudes)
    green_xc = move(green_x, "c")
    far = partial_terms(jnp.stack([green_x, green_xc]), amplitudes)

    blocks = jnp.concatenate([near, far])
    blocks = jnp.where(lax.axis_index("xh") == 1, jnp.concatenate([far, near]), blocks)
    swapped = jnp.stack([blocks[1], blocks[0], blocks[3], blocks[2]])
    blocks = jnp.where(lax.axis_index("c") == 1, swapped, blocks)
    effective = exchange(blocks, ("zh",))

    bias = jnp.dot(effective, factors, precision=HIGH, preferred_element_type=jnp.float32)
    bias = bias.reshape(4, 8, 4, 1024).transpose(2, 0, 1, 3).reshape(16, 8, 1024)
    return exchange(bias, ("xh", "c", "y0", "xl"))


def solution(mesh):
    parts = Mesh(mesh.devices.reshape(tuple(SIZES.values())), AXES)
    return jax.shard_map(
        per_device,
        mesh=parts,
        in_specs=(P(ROW, COL), P(ROW, COL), P(AXES, None)),
        out_specs=P(COL, ROW),
        check_vma=False,
    )
```

```python
import functools

import jax
import jax.numpy as jnp
from jax import lax
from jax.experimental import pallas as pl
from jax.experimental.pallas import tpu as pltpu
from jax.sharding import Mesh, PartitionSpec as P

SIZES = {"xh": 2, "c": 2, "z2": 2, "z1": 2, "z0": 2, "yh": 2, "y0": 2, "xl": 2}
AXES = tuple(SIZES)
ROW = ("xh", "c")
COL = ("z2", "z1", "z0", "yh", "y0", "xl")
VMEM_BYTES = 20 * 2**20
ALL_VMEM_BYTES = 56 * 2**20


def move(x, axis):
    return lax.ppermute(x, axis, [(0, 1), (1, 0)])


def in_order(x, other, axis):
    return jnp.where(lax.axis_index(axis) == 1, jnp.concatenate([other, x]), jnp.concatenate([x, other]))


def exchange(pieces, axes):
    return lax.all_to_all(pieces, axes, 0, 0, tiled=True)


def halves(x):
    high = x.astype(jnp.bfloat16)
    return high, (x - high.astype(jnp.float32)).astype(jnp.bfloat16)


def dot(x, y, contract):
    return lax.dot_general(x, y, (contract, ((), ())), preferred_element_type=jnp.float32)


def split_walkers(refs, walkers_ref):
    for block, ref in enumerate(refs):
        high, low = halves(ref[...])
        walkers_ref[128 * block : 128 * block + 128] = high
        walkers_ref[256 + 128 * block : 384 + 128 * block] = low


def write_terms(walkers_ref, high, low, out_ref):
    both = dot(walkers_ref[...], high, ((1,), (1,)))
    terms = both[:256] + (both[256:] + dot(walkers_ref[:256], low, ((1,), (1,))))
    for y in range(4):
        for run in range(4):
            out_ref[0, y, 16 * run : 16 * run + 16] = terms[64 * run + 16 * y : 64 * run + 16 * y + 16]


def near_kernel(green_ref, green_c_ref, amplitudes_ref, out_ref, high_ref, low_ref, walkers_ref):
    @pl.when(pl.program_id(0) == 0)
    def _():
        split_walkers((green_ref, green_c_ref), walkers_ref)

    for xl in range(2):
        for y in range(4):
            for zh in range(0, 4, 2):
                rows = jnp.concatenate([amplitudes_ref[zh, 0, y, xl], amplitudes_ref[zh + 1, 0, y, xl]])
                high, low = halves(rows)
                start = 128 * xl + 32 * y + 8 * zh
                high_ref[start : start + 16] = high
                low_ref[start : start + 16] = low
    write_terms(walkers_ref, high_ref[...], low_ref[...], out_ref)


def far_kernel(green_x_ref, green_xc_ref, high_ref, low_ref, out_ref, walkers_ref):
    @pl.when(pl.program_id(0) == 0)
    def _():
        split_walkers((green_x_ref, green_xc_ref), walkers_ref)

    write_terms(walkers_ref, high_ref[...], low_ref[...], out_ref)


def bias_kernel(effective_ref, factors_ref, out_ref):
    effective = halves(jnp.sum(effective_ref[...], axis=0))
    factors = halves(factors_ref[...])
    both = dot(jnp.concatenate(effective), factors[0], ((1,), (0,)))
    bias = both[:32] + (both[32:] + dot(effective[0], factors[1], ((1,), (0,))))
    out_ref[...] = bias.reshape(4, 8, 1024)


def near_terms(green, green_c, amplitudes):
    pairs = green.shape[1]
    walkers = pl.BlockSpec((128, pairs), lambda g: (0, 0))
    half = pl.BlockSpec((256, pairs), lambda g: (g, 0))
    halved = jax.ShapeDtypeStruct((512, pairs), jnp.bfloat16)
    return pl.pallas_call(
        near_kernel,
        out_shape=(jax.ShapeDtypeStruct((2, 4, 64, 256), jnp.float32), halved, halved),
        grid=(2,),
        in_specs=[walkers, walkers, pl.BlockSpec((4, 1, 4, 2, 8, pairs), lambda g: (0, g, 0, 0, 0, 0))],
        out_specs=(pl.BlockSpec((1, 4, 64, 256), lambda g: (g, 0, 0, 0)), half, half),
        scratch_shapes=[pltpu.VMEM((512, pairs), jnp.bfloat16)],
        compiler_params=pltpu.CompilerParams(vmem_limit_bytes=ALL_VMEM_BYTES),
        cost_estimate=pl.CostEstimate(flops=6 * 256 * 512 * pairs, bytes_accessed=11 * 2**20, transcendentals=0),
    )(green, green_c, amplitudes.reshape(4, 2, 4, 2, 8, pairs))


def far_terms(green_x, green_xc, high, low):
    pairs = green_x.shape[1]
    walkers = pl.BlockSpec((128, pairs), lambda g: (0, 0))
    half = pl.BlockSpec((256, pairs), lambda g: (g, 0))
    return pl.pallas_call(
        far_kernel,
        out_shape=jax.ShapeDtypeStruct((2, 4, 64, 256), jnp.float32),
        grid=(2,),
        in_specs=[walkers, walkers, half, half],
        out_specs=pl.BlockSpec((1, 4, 64, 256), lambda g: (g, 0, 0, 0)),
        scratch_shapes=[pltpu.VMEM((512, pairs), jnp.bfloat16)],
        compiler_params=pltpu.CompilerParams(vmem_limit_bytes=VMEM_BYTES),
        cost_estimate=pl.CostEstimate(flops=6 * 256 * 512 * pairs, bytes_accessed=6 * 2**20, transcendentals=0),
    )(green_x, green_xc, high, low)


def bias_terms(effective, factors):
    return pl.pallas_call(
        bias_kernel,
        out_shape=jax.ShapeDtypeStruct((16, 8, 1024), jnp.float32),
        grid=(4,),
        in_specs=[
            pl.BlockSpec((8, 32, 128), lambda g: (0, 0, 0)),
            pl.BlockSpec((128, 1024), lambda g: (0, g)),
        ],
        out_specs=pl.BlockSpec((4, 8, 1024), lambda g: (g, 0, 0)),
        compiler_params=pltpu.CompilerParams(vmem_limit_bytes=VMEM_BYTES),
        cost_estimate=pl.CostEstimate(flops=6 * 32 * 128 * 4096, bytes_accessed=3 * 2**20, transcendentals=0),
    )(effective, factors)


def per_device(green, amplitudes, cholesky):
    green_x = move(green, "xh")
    green_c = move(green, "c")
    other = move(cholesky, "z1")

    near, high, low = near_terms(green, green_c, amplitudes)
    near = exchange(near.reshape(8, 64, 256), ("z0", "yh", "y0"))
    high, other = lax.optimization_barrier((high, other))
    factors = in_order(cholesky, other, "z1")
    factors = in_order(factors, move(factors, "z2"), "z2")
    factors = lax.all_gather(factors, ("yh", "y0"), axis=0, tiled=True)

    near, green_x = lax.optimization_barrier((near, green_x))
    far = far_terms(green_x, move(green_x, "c"), high, low)
    far = exchange(far.reshape(8, 64, 256), ("z0", "yh", "y0"))

    near = jnp.sum(near, axis=0).reshape(2, 32, 2, 128)
    far = jnp.sum(far, axis=0).reshape(2, 32, 2, 128)
    blocks = jnp.concatenate([near, far])
    blocks = jnp.where(lax.axis_index("xh") == 1, jnp.concatenate([far, near]), blocks)
    swapped = jnp.stack([blocks[1], blocks[0], blocks[3], blocks[2]])
    blocks = jnp.where(lax.axis_index("c") == 1, swapped, blocks)
    effective = exchange(blocks.transpose(0, 2, 1, 3).reshape(8, 32, 128), ("z2", "z1", "xl"))

    bias = exchange(bias_terms(effective, factors), ("xh", "c", "z0", "xl"))
    return jnp.sum(bias, axis=0)


def solution(mesh):
    parts = Mesh(mesh.devices.reshape(tuple(SIZES.values())), AXES)
    return jax.shard_map(
        per_device,
        mesh=parts,
        in_specs=(P(ROW, COL), P(ROW, COL), P(AXES, None)),
        out_specs=P(COL, ROW),
        check_vma=False,
    )
```

```python
import functools

import jax
import jax.numpy as jnp
from jax import lax
from jax.experimental import pallas as pl
from jax.experimental.pallas import tpu as pltpu
from jax.sharding import Mesh, PartitionSpec as P

SIZES = {"xh": 2, "c": 2, "zh": 4, "z0": 2, "y": 4, "xl": 2}
AXES = tuple(SIZES)
ROW = ("xh", "c")
COL = ("zh", "z0", "y", "xl")
VMEM_BYTES = 56 * 2**20


def move(x, axis):
    return lax.ppermute(x, axis, [(0, 1), (1, 0)])


def from_above(x, axis, steps):
    return lax.ppermute(x, axis, [(i, (i - steps) % 4) for i in range(4)])


def exchange(pieces, axes):
    return lax.all_to_all(pieces, axes, 0, 0, tiled=True)


def halves(x):
    high = x.astype(jnp.bfloat16)
    return high, (x - high.astype(jnp.float32)).astype(jnp.bfloat16)


def dot(x, y, contract):
    return lax.dot_general(x, y, (contract, ((), ())), preferred_element_type=jnp.float32)


def split_walkers(refs, walkers_ref):
    for block, ref in enumerate(refs):
        high, low = halves(ref[...])
        walkers_ref[128 * block : 128 * block + 128] = high
        walkers_ref[256 + 128 * block : 384 + 128 * block] = low


def write_terms(walkers_ref, high, low, out_ref):
    both = dot(walkers_ref[...], high, ((1,), (1,)))
    terms = both[:256] + (both[256:] + dot(walkers_ref[:256], low, ((1,), (1,))))
    for y in range(4):
        for run in range(4):
            out_ref[0, y, 16 * run : 16 * run + 16] = terms[64 * run + 16 * y : 64 * run + 16 * y + 16]


def near_kernel(green_ref, green_c_ref, amplitudes_ref, out_ref, rows_ref, walkers_ref):
    @pl.when(pl.program_id(0) == 0)
    def _():
        split_walkers((green_ref, green_c_ref), walkers_ref)

    for xl in range(2):
        for y in range(4):
            for zh in range(0, 4, 2):
                rows = jnp.concatenate([amplitudes_ref[zh, 0, y, xl], amplitudes_ref[zh + 1, 0, y, xl]])
                high, low = halves(rows)
                start = 128 * xl + 32 * y + 8 * zh
                rows_ref[0, 0, start : start + 16] = high
                rows_ref[0, 1, start : start + 16] = low
    write_terms(walkers_ref, rows_ref[0, 0], rows_ref[0, 1], out_ref)


def far_kernel(green_x_ref, green_xc_ref, rows_ref, out_ref, walkers_ref):
    @pl.when(pl.program_id(0) == 0)
    def _():
        split_walkers((green_x_ref, green_xc_ref), walkers_ref)

    write_terms(walkers_ref, rows_ref[0, 0], rows_ref[0, 1], out_ref)


def bias_kernel(effective_ref, *refs):
    *factor_refs, out_ref = refs
    effective = jnp.sum(effective_ref[...], axis=0)
    effective = pltpu.roll(effective, lax.rem(128 - 32 * lax.axis_index("y"), 128), 1)
    shift = 8 * lax.axis_index("zh")
    lane = lax.broadcasted_iota(jnp.int32, effective.shape, 1)
    effective = jnp.where(
        lax.rem(lane, 32) < 32 - shift,
        pltpu.roll(effective, lax.rem(128 - shift, 128), 1),
        pltpu.roll(effective, 32 - shift, 1),
    )
    high, low = halves(effective)
    own, up, left, right, down = [halves(ref[...]) for ref in factor_refs]
    across = [jnp.concatenate(pair, axis=1) for pair in zip(left, right)]
    parts = [own, up, across, down]
    both = dot(jnp.concatenate([high, low]), jnp.concatenate([part[0] for part in parts]), ((1,), (0,)))
    cross = dot(high, jnp.concatenate([part[1] for part in parts]), ((1,), (0,)))
    bias = (both[:32] + (both[32:] + cross)).reshape(4, 8, 4096)
    for g in range(4):
        out_ref[4 * g : 4 * g + 4] = bias[:, :, 1024 * g : 1024 * g + 1024]


def near_terms(green, green_c, amplitudes):
    pairs = green.shape[1]
    walkers = pl.BlockSpec((128, pairs), lambda g: (0, 0))
    return pl.pallas_call(
        near_kernel,
        out_shape=(
            jax.ShapeDtypeStruct((2, 4, 64, 256), jnp.float32),
            jax.ShapeDtypeStruct((2, 2, 256, pairs), jnp.bfloat16),
        ),
        grid=(2,),
        in_specs=[walkers, walkers, pl.BlockSpec((4, 1, 4, 2, 8, pairs), lambda g: (0, g, 0, 0, 0, 0))],
        out_specs=(
            pl.BlockSpec((1, 4, 64, 256), lambda g: (g, 0, 0, 0)),
            pl.BlockSpec((1, 2, 256, pairs), lambda g: (g, 0, 0, 0)),
        ),
        scratch_shapes=[pltpu.VMEM((512, pairs), jnp.bfloat16)],
        compiler_params=pltpu.CompilerParams(vmem_limit_bytes=VMEM_BYTES),
        cost_estimate=pl.CostEstimate(flops=0, bytes_accessed=0, transcendentals=0),
    )(green, green_c, amplitudes.reshape(4, 2, 4, 2, 8, pairs))


def far_terms(green_x, green_xc, rows):
    pairs = green_x.shape[1]
    walkers = pl.BlockSpec((128, pairs), lambda g: (0, 0))
    return pl.pallas_call(
        far_kernel,
        out_shape=jax.ShapeDtypeStruct((2, 4, 64, 256), jnp.float32),
        grid=(2,),
        in_specs=[walkers, walkers, pl.BlockSpec((1, 2, 256, pairs), lambda g: (g, 0, 0, 0))],
        out_specs=pl.BlockSpec((1, 4, 64, 256), lambda g: (g, 0, 0, 0)),
        scratch_shapes=[pltpu.VMEM((512, pairs), jnp.bfloat16)],
        compiler_params=pltpu.CompilerParams(vmem_limit_bytes=20 * 2**20),
        cost_estimate=pl.CostEstimate(flops=0, bytes_accessed=0, transcendentals=0),
    )(green_x, green_xc, rows)


def bias_terms(effective, factors):
    return pl.pallas_call(
        bias_kernel,
        out_shape=jax.ShapeDtypeStruct((16, 8, 1024), jnp.float32),
        grid=(1,),
        in_specs=[pl.BlockSpec((8, 32, 128), lambda g: (0, 0, 0))] + [pl.BlockSpec(factor.shape, lambda g: (0, 0)) for factor in factors],
        out_specs=pl.BlockSpec((16, 8, 1024), lambda g: (0, 0, 0)),
        compiler_params=pltpu.CompilerParams(vmem_limit_bytes=VMEM_BYTES),
        cost_estimate=pl.CostEstimate(flops=6 * 32 * 128 * 4096, bytes_accessed=3 * 2**20, transcendentals=0),
    )(effective, *factors)


def per_device(green, amplitudes, cholesky):
    green_x = move(green, "xh")
    green_c = move(green, "c")
    others = [from_above(cholesky, "zh", k) for k in (1, 2, 3)]

    near, rows = near_terms(green, green_c, amplitudes)
    near = exchange(near.reshape(8, 64, 256), ("z0", "y"))
    owned = jnp.concatenate([cholesky] + others)
    up, down = from_above(owned, "y", 1), from_above(owned, "y", 3)
    near, green_x, owned = lax.optimization_barrier((near, green_x, owned))
    far = far_terms(green_x, move(green_x, "c"), rows)
    far, up, down = lax.optimization_barrier((far, up, down))
    left, right = from_above(up[:, :2048], "y", 1), from_above(down[:, 2048:], "y", 3)
    far = exchange(far.reshape(8, 64, 256), ("z0", "y"))
    factors = [owned, up, left, right, down]

    near = jnp.sum(near, axis=0).reshape(2, 32, 2, 128)
    far = jnp.sum(far, axis=0).reshape(2, 32, 2, 128)
    blocks = jnp.concatenate([near, far])
    blocks = jnp.where(lax.axis_index("xh") == 1, jnp.concatenate([far, near]), blocks)
    swapped = jnp.stack([blocks[1], blocks[0], blocks[3], blocks[2]])
    blocks = jnp.where(lax.axis_index("c") == 1, swapped, blocks)
    effective = exchange(blocks.transpose(0, 2, 1, 3).reshape(8, 32, 128), ("zh", "xl"))

    bias = exchange(bias_terms(effective, factors), ("xh", "c", "z0", "xl"))
    return jnp.sum(bias, axis=0)


def solution(mesh):
    parts = Mesh(mesh.devices.reshape(tuple(SIZES.values())), AXES)
    return jax.shard_map(
        per_device,
        mesh=parts,
        in_specs=(P(ROW, COL), P(ROW, COL), P(AXES, None)),
        out_specs=P(COL, ROW),
        check_vma=False,
    )
```

```python
import functools

import jax
import jax.numpy as jnp
from jax import lax
from jax.experimental import pallas as pl
from jax.experimental.pallas import tpu as pltpu
from jax.sharding import Mesh, PartitionSpec as P

SIZES = {"xh": 2, "c": 2, "zh": 4, "z0": 2, "y": 4, "xl": 2}
AXES = tuple(SIZES)
ROW = ("xh", "c")
COL = ("zh", "z0", "y", "xl")
VMEM_BYTES = 56 * 2**20


def move(x, axis):
    return lax.ppermute(x, axis, [(0, 1), (1, 0)])


def from_above(x, axis, steps):
    return lax.ppermute(x, axis, [(i, (i - steps) % 4) for i in range(4)])


def exchange(pieces, axes):
    return lax.all_to_all(pieces, axes, 0, 0, tiled=True)


def halves(x):
    high = x.astype(jnp.bfloat16)
    return high, (x - high.astype(jnp.float32)).astype(jnp.bfloat16)


def dot(x, y, contract):
    return lax.dot_general(x, y, (contract, ((), ())), preferred_element_type=jnp.float32)


def split_walkers(refs, walkers_ref):
    for block, ref in enumerate(refs):
        high, low = halves(ref[...])
        walkers_ref[128 * block : 128 * block + 128] = high
        walkers_ref[256 + 128 * block : 384 + 128 * block] = low


def write_terms(walkers_ref, high, low, out_ref):
    both = dot(walkers_ref[...], high, ((1,), (1,)))
    terms = both[:256] + (both[256:] + dot(walkers_ref[:256], low, ((1,), (1,))))
    for y in range(4):
        for run in range(4):
            out_ref[0, y, 16 * run : 16 * run + 16] = terms[64 * run + 16 * y : 64 * run + 16 * y + 16]


def near_kernel(green_ref, green_c_ref, amplitudes_ref, out_ref, rows_ref, walkers_ref):
    @pl.when(pl.program_id(0) == 0)
    def _():
        split_walkers((green_ref, green_c_ref), walkers_ref)

    for xl in range(2):
        for y in range(4):
            for zh in range(0, 4, 2):
                rows = jnp.concatenate([amplitudes_ref[zh, 0, y, xl], amplitudes_ref[zh + 1, 0, y, xl]])
                high, low = halves(rows)
                start = 128 * xl + 32 * y + 8 * zh
                rows_ref[0, 0, start : start + 16] = high
                rows_ref[0, 1, start : start + 16] = low
    write_terms(walkers_ref, rows_ref[0, 0], rows_ref[0, 1], out_ref)


def far_kernel(green_x_ref, green_xc_ref, rows_ref, out_ref, walkers_ref):
    @pl.when(pl.program_id(0) == 0)
    def _():
        split_walkers((green_x_ref, green_xc_ref), walkers_ref)

    write_terms(walkers_ref, rows_ref[0, 0], rows_ref[0, 1], out_ref)


def bias_kernel(effective_ref, *refs):
    *factor_refs, mine_ref, theirs_ref = refs
    effective = jnp.sum(effective_ref[...], axis=0)
    effective = pltpu.roll(effective, lax.rem(128 - 32 * lax.axis_index("y"), 128), 1)
    shift = 8 * lax.axis_index("zh")
    lane = lax.broadcasted_iota(jnp.int32, effective.shape, 1)
    effective = jnp.where(
        lax.rem(lane, 32) < 32 - shift,
        pltpu.roll(effective, lax.rem(128 - shift, 128), 1),
        pltpu.roll(effective, 32 - shift, 1),
    )
    high, low = halves(effective)
    own, up, left, right, down = [halves(ref[...]) for ref in factor_refs]
    across = [jnp.concatenate(pair, axis=1) for pair in zip(left, right)]
    parts = [own, up, across, down]
    both = dot(jnp.concatenate([high, low]), jnp.concatenate([part[0] for part in parts]), ((1,), (0,)))
    cross = dot(high, jnp.concatenate([part[1] for part in parts]), ((1,), (0,)))
    bias = (both[:32] + (both[32:] + cross)).reshape(4, 8, 4096)
    for core in range(2):

        @pl.when(lax.axis_index("c") == core)
        def _():
            for xh in range(2):
                for ref, to in ((mine_ref, core), (theirs_ref, 1 - core)):
                    start = 1024 * (2 * xh + to)
                    ref[4 * xh : 4 * xh + 4] = bias[:, :, start : start + 1024]


def near_terms(green, green_c, amplitudes):
    pairs = green.shape[1]
    walkers = pl.BlockSpec((128, pairs), lambda g: (0, 0))
    return pl.pallas_call(
        near_kernel,
        out_shape=(
            jax.ShapeDtypeStruct((2, 4, 64, 256), jnp.float32),
            jax.ShapeDtypeStruct((2, 2, 256, pairs), jnp.bfloat16),
        ),
        grid=(2,),
        in_specs=[walkers, walkers, pl.BlockSpec((4, 1, 4, 2, 8, pairs), lambda g: (0, g, 0, 0, 0, 0))],
        out_specs=(
            pl.BlockSpec((1, 4, 64, 256), lambda g: (g, 0, 0, 0)),
            pl.BlockSpec((1, 2, 256, pairs), lambda g: (g, 0, 0, 0)),
        ),
        scratch_shapes=[pltpu.VMEM((512, pairs), jnp.bfloat16)],
        compiler_params=pltpu.CompilerParams(vmem_limit_bytes=VMEM_BYTES),
        cost_estimate=pl.CostEstimate(flops=0, bytes_accessed=0, transcendentals=0),
    )(green, green_c, amplitudes.reshape(4, 2, 4, 2, 8, pairs))


def far_terms(green_x, green_xc, rows):
    pairs = green_x.shape[1]
    walkers = pl.BlockSpec((128, pairs), lambda g: (0, 0))
    return pl.pallas_call(
        far_kernel,
        out_shape=jax.ShapeDtypeStruct((2, 4, 64, 256), jnp.float32),
        grid=(2,),
        in_specs=[walkers, walkers, pl.BlockSpec((1, 2, 256, pairs), lambda g: (g, 0, 0, 0))],
        out_specs=pl.BlockSpec((1, 4, 64, 256), lambda g: (g, 0, 0, 0)),
        scratch_shapes=[pltpu.VMEM((512, pairs), jnp.bfloat16)],
        compiler_params=pltpu.CompilerParams(vmem_limit_bytes=20 * 2**20),
        cost_estimate=pl.CostEstimate(flops=0, bytes_accessed=0, transcendentals=0),
    )(green_x, green_xc, rows)


def bias_terms(effective, factors):
    whole = pl.BlockSpec(memory_space=pltpu.VMEM)
    piece = jax.ShapeDtypeStruct((8, 8, 1024), jnp.float32)
    return pl.pallas_call(
        bias_kernel,
        out_shape=(piece, piece),
        in_specs=[whole] * (1 + len(factors)),
        out_specs=(whole, whole),
        compiler_params=pltpu.CompilerParams(vmem_limit_bytes=16 * 2**20),
        cost_estimate=pl.CostEstimate(flops=6 * 32 * 128 * 4096, bytes_accessed=3 * 2**20, transcendentals=0),
    )(effective, *factors)


def by_row_part(terms):
    return jnp.stack([terms[:, :128].reshape(2, 32, 128), terms[:, 128:].reshape(2, 32, 128)], axis=1)


def per_device(green, amplitudes, cholesky):
    green_x = move(green, "xh")
    green_c = move(green, "c")
    others = [from_above(cholesky, "zh", k) for k in (1, 2, 3)]

    near, rows = near_terms(green, green_c, amplitudes)
    near = exchange(near.reshape(8, 64, 256), ("z0", "y"))
    owned = jnp.concatenate([cholesky] + others)
    up, down = from_above(owned, "y", 1), from_above(owned, "y", 3)
    near, green_x, owned = lax.optimization_barrier((near, green_x, owned))
    far = far_terms(green_x, move(green_x, "c"), rows)
    far, up, down = lax.optimization_barrier((far, up, down))
    left, right = from_above(up[:, :2048], "y", 1), from_above(down[:, 2048:], "y", 3)
    far = exchange(far.reshape(8, 64, 256), ("z0", "y"))
    factors = [owned, up, left, right, down]

    near, far = by_row_part(jnp.sum(near, axis=0)), by_row_part(jnp.sum(far, axis=0))
    blocks = jnp.concatenate([near, far])
    blocks = jnp.where(lax.axis_index("xh") == 1, jnp.concatenate([far, near]), blocks)
    swapped = jnp.stack([blocks[1], blocks[0], blocks[3], blocks[2]])
    blocks = jnp.where(lax.axis_index("c") == 1, swapped, blocks)
    effective = exchange(blocks.reshape(8, 32, 128), ("zh", "xl"))

    mine, theirs = bias_terms(effective, factors)
    bias = exchange(mine + move(theirs, "c"), ("xh", "z0", "xl"))
    return jnp.sum(bias, axis=0)


def solution(mesh):
    parts = Mesh(mesh.devices.reshape(tuple(SIZES.values())), AXES)
    return jax.shard_map(
        per_device,
        mesh=parts,
        in_specs=(P(ROW, COL), P(ROW, COL), P(AXES, None)),
        out_specs=P(COL, ROW),
        check_vma=False,
    )
```

```python
import functools

import jax
import jax.numpy as jnp
from jax import lax
from jax.experimental import pallas as pl
from jax.experimental.pallas import tpu as pltpu
from jax.sharding import Mesh, PartitionSpec as P

SIZES = {"xh": 2, "c": 2, "zh": 4, "z0": 2, "y": 4, "xl": 2}
AXES = tuple(SIZES)
ROW = ("xh", "c")
COL = ("zh", "z0", "y", "xl")
VMEM_BYTES = 56 * 2**20


def move(x, axis):
    return lax.ppermute(x, axis, [(0, 1), (1, 0)])


def from_above(x, axis, steps):
    return lax.ppermute(x, axis, [(i, (i - steps) % 4) for i in range(4)])


def exchange(pieces, axes):
    return lax.all_to_all(pieces, axes, 0, 0, tiled=True)


def halves(x):
    high = x.astype(jnp.bfloat16)
    return high, (x - high.astype(jnp.float32)).astype(jnp.bfloat16)


def dot(x, y, contract):
    return lax.dot_general(x, y, (contract, ((), ())), preferred_element_type=jnp.float32)


def split_walkers(refs, walkers_ref):
    for block, ref in enumerate(refs):
        high, low = halves(ref[...])
        walkers_ref[128 * block : 128 * block + 128] = high
        walkers_ref[256 + 128 * block : 384 + 128 * block] = low


def write_terms(walkers_ref, high, low, out_ref):
    both = dot(walkers_ref[...], high, ((1,), (1,)))
    terms = both[:256] + (both[256:] + dot(walkers_ref[:256], low, ((1,), (1,))))
    for y in range(4):
        for run in range(4):
            out_ref[0, y, 16 * run : 16 * run + 16] = terms[64 * run + 16 * y : 64 * run + 16 * y + 16]


def near_kernel(green_ref, green_c_ref, amplitudes_ref, out_ref, rows_ref, walkers_ref):
    @pl.when(pl.program_id(0) == 0)
    def _():
        split_walkers((green_ref, green_c_ref), walkers_ref)

    for xl in range(2):
        for y in range(4):
            for zh in range(0, 4, 2):
                rows = jnp.concatenate([amplitudes_ref[zh, 0, y, xl], amplitudes_ref[zh + 1, 0, y, xl]])
                high, low = halves(rows)
                start = 128 * xl + 32 * y + 8 * zh
                rows_ref[0, 0, start : start + 16] = high
                rows_ref[0, 1, start : start + 16] = low
    write_terms(walkers_ref, rows_ref[0, 0], rows_ref[0, 1], out_ref)


def far_kernel(green_x_ref, green_xc_ref, rows_ref, out_ref, walkers_ref):
    @pl.when(pl.program_id(0) == 0)
    def _():
        split_walkers((green_x_ref, green_xc_ref), walkers_ref)

    write_terms(walkers_ref, rows_ref[0, 0], rows_ref[0, 1], out_ref)


def bias_kernel(effective_ref, *refs):
    *factor_refs, mine_ref, theirs_ref = refs
    effective = jnp.sum(effective_ref[...], axis=0)
    effective = pltpu.roll(effective, lax.rem(128 - 32 * lax.axis_index("y"), 128), 1)
    shift = 8 * lax.axis_index("zh")
    lane = lax.broadcasted_iota(jnp.int32, effective.shape, 1)
    effective = jnp.where(
        lax.rem(lane, 32) < 32 - shift,
        pltpu.roll(effective, lax.rem(128 - shift, 128), 1),
        pltpu.roll(effective, 32 - shift, 1),
    )
    high, low = halves(effective)
    own, up, left, right, down = [halves(ref[...]) for ref in factor_refs]
    across = [jnp.concatenate(pair, axis=1) for pair in zip(left, right)]
    parts = [own, up, across, down]
    both = dot(jnp.concatenate([high, low]), jnp.concatenate([part[0] for part in parts]), ((1,), (0,)))
    cross = dot(high, jnp.concatenate([part[1] for part in parts]), ((1,), (0,)))
    bias = (both[:32] + (both[32:] + cross)).reshape(4, 8, 4096)
    for core in range(2):

        @pl.when(lax.axis_index("c") == core)
        def _():
            for xh in range(2):
                for ref, to in ((mine_ref, core), (theirs_ref, 1 - core)):
                    start = 1024 * (2 * xh + to)
                    ref[4 * xh : 4 * xh + 4] = bias[:, :, start : start + 1024]


def near_terms(green, green_c, amplitudes):
    pairs = green.shape[1]
    walkers = pl.BlockSpec((128, pairs), lambda g: (0, 0))
    return pl.pallas_call(
        near_kernel,
        out_shape=(
            jax.ShapeDtypeStruct((2, 4, 64, 256), jnp.float32),
            jax.ShapeDtypeStruct((2, 2, 256, pairs), jnp.bfloat16),
        ),
        grid=(2,),
        in_specs=[walkers, walkers, pl.BlockSpec((4, 1, 4, 2, 8, pairs), lambda g: (0, g, 0, 0, 0, 0))],
        out_specs=(
            pl.BlockSpec((1, 4, 64, 256), lambda g: (g, 0, 0, 0)),
            pl.BlockSpec((1, 2, 256, pairs), lambda g: (g, 0, 0, 0)),
        ),
        scratch_shapes=[pltpu.VMEM((512, pairs), jnp.bfloat16)],
        compiler_params=pltpu.CompilerParams(vmem_limit_bytes=VMEM_BYTES),
        cost_estimate=pl.CostEstimate(flops=0, bytes_accessed=0, transcendentals=0),
    )(green, green_c, amplitudes.reshape(4, 2, 4, 2, 8, pairs))


def far_terms(green_x, green_xc, rows):
    pairs = green_x.shape[1]
    walkers = pl.BlockSpec((128, pairs), lambda g: (0, 0))
    return pl.pallas_call(
        far_kernel,
        out_shape=jax.ShapeDtypeStruct((2, 4, 64, 256), jnp.float32),
        grid=(2,),
        in_specs=[walkers, walkers, pl.BlockSpec((1, 2, 256, pairs), lambda g: (g, 0, 0, 0))],
        out_specs=pl.BlockSpec((1, 4, 64, 256), lambda g: (g, 0, 0, 0)),
        scratch_shapes=[pltpu.VMEM((512, pairs), jnp.bfloat16)],
        compiler_params=pltpu.CompilerParams(vmem_limit_bytes=20 * 2**20),
        cost_estimate=pl.CostEstimate(flops=0, bytes_accessed=0, transcendentals=0),
    )(green_x, green_xc, rows)


def bias_terms(effective, factors):
    whole = pl.BlockSpec(memory_space=pltpu.VMEM)
    piece = jax.ShapeDtypeStruct((8, 8, 1024), jnp.float32)
    return pl.pallas_call(
        bias_kernel,
        out_shape=(piece, piece),
        in_specs=[whole] * (1 + len(factors)),
        out_specs=(whole, whole),
        compiler_params=pltpu.CompilerParams(vmem_limit_bytes=16 * 2**20),
        cost_estimate=pl.CostEstimate(flops=6 * 32 * 128 * 4096, bytes_accessed=3 * 2**20, transcendentals=0),
    )(effective, *factors)


def by_row_part(terms):
    return jnp.stack([terms[:, :128].reshape(2, 32, 128), terms[:, 128:].reshape(2, 32, 128)], axis=1)


def per_device(green, amplitudes, cholesky):
    green_x = move(green, "xh")
    green_c = move(green, "c")
    others = [from_above(cholesky, "zh", k) for k in (1, 2, 3)]

    near, rows = near_terms(green, green_c, amplitudes)
    near = exchange(near.reshape(8, 64, 256), ("z0", "y"))
    owned = jnp.concatenate([cholesky] + others)
    up, down = from_above(owned, "y", 1), from_above(owned, "y", 3)
    near, green_x, owned = lax.optimization_barrier((near, green_x, owned))
    far = far_terms(green_x, move(green_x, "c"), rows)
    far, up, down = lax.optimization_barrier((far, up, down))
    far = exchange(far.reshape(8, 64, 256), ("z0", "y"))
    far, up, down = lax.optimization_barrier((far, up, down))
    left, right = from_above(up[:, :2048], "y", 1), from_above(down[:, 2048:], "y", 3)
    factors = [owned, up, left, right, down]

    near, far = by_row_part(jnp.sum(near, axis=0)), by_row_part(jnp.sum(far, axis=0))
    blocks = jnp.concatenate([near, far])
    blocks = jnp.where(lax.axis_index("xh") == 1, jnp.concatenate([far, near]), blocks)
    swapped = jnp.stack([blocks[1], blocks[0], blocks[3], blocks[2]])
    blocks = jnp.where(lax.axis_index("c") == 1, swapped, blocks)
    effective = exchange(blocks.reshape(8, 32, 128), ("zh", "xl"))

    mine, theirs = bias_terms(effective, factors)
    bias = exchange(mine + move(theirs, "c"), ("xh", "z0", "xl"))
    return jnp.sum(bias, axis=0)


def solution(mesh):
    parts = Mesh(mesh.devices.reshape(tuple(SIZES.values())), AXES)
    return jax.shard_map(
        per_device,
        mesh=parts,
        in_specs=(P(ROW, COL), P(ROW, COL), P(AXES, None)),
        out_specs=P(COL, ROW),
        check_vma=False,
    )
```

```python
import functools

import jax
import jax.numpy as jnp
from jax import lax
from jax.experimental import pallas as pl
from jax.experimental.pallas import tpu as pltpu
from jax.sharding import Mesh, PartitionSpec as P

SIZES = {"xh": 2, "c": 2, "zh": 4, "z0": 2, "y": 4, "xl": 2}
AXES = tuple(SIZES)
ROW = ("xh", "c")
COL = ("zh", "z0", "y", "xl")
VMEM_BYTES = 56 * 2**20


def move(x, axis):
    return lax.ppermute(x, axis, [(0, 1), (1, 0)])


def from_above(x, axis, steps):
    return lax.ppermute(x, axis, [(i, (i - steps) % 4) for i in range(4)])


def exchange(pieces, axes):
    return lax.all_to_all(pieces, axes, 0, 0, tiled=True)


def halves(x):
    high = x.astype(jnp.bfloat16)
    return high, (x - high.astype(jnp.float32)).astype(jnp.bfloat16)


def dot(x, y, contract):
    return lax.dot_general(x, y, (contract, ((), ())), preferred_element_type=jnp.float32)


def split_walkers(refs, walkers_ref):
    for block, ref in enumerate(refs):
        high, low = halves(ref[...])
        walkers_ref[128 * block : 128 * block + 128] = high
        walkers_ref[256 + 128 * block : 384 + 128 * block] = low


def write_terms(walkers_ref, high, low, out_ref):
    both = dot(walkers_ref[...], high, ((1,), (1,)))
    terms = both[:256] + (both[256:] + dot(walkers_ref[:256], low, ((1,), (1,))))
    for y in range(4):
        for run in range(4):
            out_ref[0, y, 16 * run : 16 * run + 16] = terms[64 * run + 16 * y : 64 * run + 16 * y + 16]


def near_kernel(green_ref, green_c_ref, amplitudes_ref, out_ref, rows_ref, walkers_ref):
    @pl.when(pl.program_id(0) == 0)
    def _():
        split_walkers((green_ref, green_c_ref), walkers_ref)

    for xl in range(2):
        for y in range(4):
            for zh in range(0, 4, 2):
                rows = jnp.concatenate([amplitudes_ref[zh, 0, y, xl], amplitudes_ref[zh + 1, 0, y, xl]])
                high, low = halves(rows)
                start = 128 * xl + 32 * y + 8 * zh
                rows_ref[0, 0, start : start + 16] = high
                rows_ref[0, 1, start : start + 16] = low
    write_terms(walkers_ref, rows_ref[0, 0], rows_ref[0, 1], out_ref)


def far_kernel(green_x_ref, green_xc_ref, rows_ref, out_ref, walkers_ref):
    @pl.when(pl.program_id(0) == 0)
    def _():
        split_walkers((green_x_ref, green_xc_ref), walkers_ref)

    write_terms(walkers_ref, rows_ref[0, 0], rows_ref[0, 1], out_ref)


def bias_kernel(effective_ref, *refs):
    *factor_refs, mine_ref, theirs_ref = refs
    effective = jnp.sum(effective_ref[...], axis=0)
    effective = pltpu.roll(effective, lax.rem(128 - 32 * lax.axis_index("y"), 128), 1)
    shift = 8 * lax.axis_index("zh")
    lane = lax.broadcasted_iota(jnp.int32, effective.shape, 1)
    effective = jnp.where(
        lax.rem(lane, 32) < 32 - shift,
        pltpu.roll(effective, lax.rem(128 - shift, 128), 1),
        pltpu.roll(effective, 32 - shift, 1),
    )
    high, low = halves(effective)
    own, up, *across, down = [halves(ref[...]) for ref in factor_refs]
    across = [jnp.concatenate(quarters, axis=1) for quarters in zip(*across)]
    parts = [own, up, across, down]
    both = dot(jnp.concatenate([high, low]), jnp.concatenate([part[0] for part in parts]), ((1,), (0,)))
    cross = dot(high, jnp.concatenate([part[1] for part in parts]), ((1,), (0,)))
    bias = (both[:32] + (both[32:] + cross)).reshape(4, 8, 4096)
    for core in range(2):

        @pl.when(lax.axis_index("c") == core)
        def _():
            for xh in range(2):
                for ref, to in ((mine_ref, core), (theirs_ref, 1 - core)):
                    start = 1024 * (2 * xh + to)
                    ref[4 * xh : 4 * xh + 4] = bias[:, :, start : start + 1024]


def near_terms(green, green_c, amplitudes):
    pairs = green.shape[1]
    walkers = pl.BlockSpec((128, pairs), lambda g: (0, 0))
    return pl.pallas_call(
        near_kernel,
        out_shape=(
            jax.ShapeDtypeStruct((2, 4, 64, 256), jnp.float32),
            jax.ShapeDtypeStruct((2, 2, 256, pairs), jnp.bfloat16),
        ),
        grid=(2,),
        in_specs=[walkers, walkers, pl.BlockSpec((4, 1, 4, 2, 8, pairs), lambda g: (0, g, 0, 0, 0, 0))],
        out_specs=(
            pl.BlockSpec((1, 4, 64, 256), lambda g: (g, 0, 0, 0)),
            pl.BlockSpec((1, 2, 256, pairs), lambda g: (g, 0, 0, 0)),
        ),
        scratch_shapes=[pltpu.VMEM((512, pairs), jnp.bfloat16)],
        compiler_params=pltpu.CompilerParams(vmem_limit_bytes=VMEM_BYTES),
        cost_estimate=pl.CostEstimate(flops=0, bytes_accessed=0, transcendentals=0),
    )(green, green_c, amplitudes.reshape(4, 2, 4, 2, 8, pairs))


def far_terms(green_x, green_xc, rows):
    pairs = green_x.shape[1]
    walkers = pl.BlockSpec((128, pairs), lambda g: (0, 0))
    return pl.pallas_call(
        far_kernel,
        out_shape=jax.ShapeDtypeStruct((2, 4, 64, 256), jnp.float32),
        grid=(2,),
        in_specs=[walkers, walkers, pl.BlockSpec((1, 2, 256, pairs), lambda g: (g, 0, 0, 0))],
        out_specs=pl.BlockSpec((1, 4, 64, 256), lambda g: (g, 0, 0, 0)),
        scratch_shapes=[pltpu.VMEM((512, pairs), jnp.bfloat16)],
        compiler_params=pltpu.CompilerParams(vmem_limit_bytes=20 * 2**20),
        cost_estimate=pl.CostEstimate(flops=0, bytes_accessed=0, transcendentals=0),
    )(green_x, green_xc, rows)


def bias_terms(effective, factors):
    whole = pl.BlockSpec(memory_space=pltpu.VMEM)
    piece = jax.ShapeDtypeStruct((8, 8, 1024), jnp.float32)
    return pl.pallas_call(
        bias_kernel,
        out_shape=(piece, piece),
        in_specs=[whole] * (1 + len(factors)),
        out_specs=(whole, whole),
        compiler_params=pltpu.CompilerParams(vmem_limit_bytes=16 * 2**20),
        cost_estimate=pl.CostEstimate(flops=6 * 32 * 128 * 4096, bytes_accessed=3 * 2**20, transcendentals=0),
    )(effective, *factors)


def by_row_part(terms):
    return jnp.stack([terms[:, :128].reshape(2, 32, 128), terms[:, 128:].reshape(2, 32, 128)], axis=1)


def per_device(green, amplitudes, cholesky):
    green_x = move(green, "xh")
    green_c = move(green, "c")
    others = [from_above(cholesky, "zh", k) for k in (1, 2, 3)]

    near, rows = near_terms(green, green_c, amplitudes)
    near = exchange(near.reshape(8, 64, 256), ("z0", "y"))
    owned = jnp.concatenate([cholesky] + others)
    up, down = from_above(owned, "y", 1), from_above(owned, "y", 3)
    near, green_x, owned = lax.optimization_barrier((near, green_x, owned))
    far = far_terms(green_x, move(green_x, "c"), rows)
    far, up, down = lax.optimization_barrier((far, up, down))
    far = exchange(far.reshape(8, 64, 256), ("z0", "y"))
    far, up, down = lax.optimization_barrier((far, up, down))
    across = [from_above(up[:, 1024 * k : 1024 * k + 1024], "y", 1) for k in (0, 1)]
    across += [from_above(down[:, 1024 * k : 1024 * k + 1024], "y", 3) for k in (2, 3)]
    factors = [owned, up, *across, down]

    near, far = by_row_part(jnp.sum(near, axis=0)), by_row_part(jnp.sum(far, axis=0))
    blocks = jnp.concatenate([near, far])
    blocks = jnp.where(lax.axis_index("xh") == 1, jnp.concatenate([far, near]), blocks)
    swapped = jnp.stack([blocks[1], blocks[0], blocks[3], blocks[2]])
    blocks = jnp.where(lax.axis_index("c") == 1, swapped, blocks)
    effective = exchange(blocks.reshape(8, 32, 128), ("zh", "xl"))

    mine, theirs = bias_terms(effective, factors)
    bias = exchange(mine + move(theirs, "c"), ("xh", "z0", "xl"))
    return jnp.sum(bias, axis=0)


def solution(mesh):
    parts = Mesh(mesh.devices.reshape(tuple(SIZES.values())), AXES)
    return jax.shard_map(
        per_device,
        mesh=parts,
        in_specs=(P(ROW, COL), P(ROW, COL), P(AXES, None)),
        out_specs=P(COL, ROW),
        check_vma=False,
    )
```

```python
import functools

import jax
import jax.numpy as jnp
from jax import lax
from jax.experimental import pallas as pl
from jax.experimental.pallas import tpu as pltpu
from jax.sharding import Mesh, PartitionSpec as P

SIZES = {"xh": 2, "c": 2, "zh": 4, "z0": 2, "y": 4, "xl": 2}
AXES = tuple(SIZES)
ROW = ("xh", "c")
COL = ("zh", "z0", "y", "xl")
VMEM_BYTES = 56 * 2**20


def move(x, axis):
    return lax.ppermute(x, axis, [(0, 1), (1, 0)])


def from_above(x, axis, steps):
    return lax.ppermute(x, axis, [(i, (i - steps) % 4) for i in range(4)])


def exchange(pieces, axes):
    return lax.all_to_all(pieces, axes, 0, 0, tiled=True)


def halves(x):
    high = x.astype(jnp.bfloat16)
    return high, (x - high.astype(jnp.float32)).astype(jnp.bfloat16)


def dot(x, y, contract):
    return lax.dot_general(x, y, (contract, ((), ())), preferred_element_type=jnp.float32)


def split_walkers(refs, walkers_ref):
    for block, ref in enumerate(refs):
        high, low = halves(ref[...])
        walkers_ref[128 * block : 128 * block + 128] = high
        walkers_ref[256 + 128 * block : 384 + 128 * block] = low


def write_terms(walkers_ref, high, low, out_ref):
    both = dot(walkers_ref[...], high, ((1,), (1,)))
    terms = both[:256] + (both[256:] + dot(walkers_ref[:256], low, ((1,), (1,))))
    for y in range(4):
        for run in range(4):
            out_ref[0, y, 16 * run : 16 * run + 16] = terms[64 * run + 16 * y : 64 * run + 16 * y + 16]


def near_kernel(green_ref, green_c_ref, amplitudes_ref, out_ref, rows_ref, walkers_ref):
    @pl.when(pl.program_id(0) == 0)
    def _():
        split_walkers((green_ref, green_c_ref), walkers_ref)

    for xl in range(2):
        for y in range(4):
            for zh in range(0, 4, 2):
                rows = jnp.concatenate([amplitudes_ref[zh, 0, y, xl], amplitudes_ref[zh + 1, 0, y, xl]])
                high, low = halves(rows)
                start = 128 * xl + 32 * y + 8 * zh
                rows_ref[0, 0, start : start + 16] = high
                rows_ref[0, 1, start : start + 16] = low
    write_terms(walkers_ref, rows_ref[0, 0], rows_ref[0, 1], out_ref)


def far_kernel(green_x_ref, green_xc_ref, rows_ref, out_ref, walkers_ref):
    @pl.when(pl.program_id(0) == 0)
    def _():
        split_walkers((green_x_ref, green_xc_ref), walkers_ref)

    write_terms(walkers_ref, rows_ref[0, 0], rows_ref[0, 1], out_ref)


def bias_kernel(effective_ref, *refs):
    *factor_refs, mine_ref, theirs_ref = refs
    effective = jnp.sum(effective_ref[...], axis=0)
    effective = pltpu.roll(effective, lax.rem(128 - 32 * lax.axis_index("y"), 128), 1)
    shift = 8 * lax.axis_index("zh")
    lane = lax.broadcasted_iota(jnp.int32, effective.shape, 1)
    effective = jnp.where(
        lax.rem(lane, 32) < 32 - shift,
        pltpu.roll(effective, lax.rem(128 - shift, 128), 1),
        pltpu.roll(effective, 32 - shift, 1),
    )
    high, low = halves(effective)
    own, up, left, right, down = [halves(ref[...]) for ref in factor_refs]
    across = [jnp.concatenate(pair, axis=1) for pair in zip(left, right)]
    parts = [own, up, across, down]
    both = dot(jnp.concatenate([high, low]), jnp.concatenate([part[0] for part in parts]), ((1,), (0,)))
    cross = dot(high, jnp.concatenate([part[1] for part in parts]), ((1,), (0,)))
    bias = (both[:32] + (both[32:] + cross)).reshape(4, 8, 4096)
    for core in range(2):

        @pl.when(lax.axis_index("c") == core)
        def _():
            for xh in range(2):
                for ref, to in ((mine_ref, core), (theirs_ref, 1 - core)):
                    start = 1024 * (2 * xh + to)
                    ref[4 * xh : 4 * xh + 4] = bias[:, :, start : start + 1024]


def near_terms(green, green_c, amplitudes):
    pairs = green.shape[1]
    walkers = pl.BlockSpec((128, pairs), lambda g: (0, 0))
    return pl.pallas_call(
        near_kernel,
        out_shape=(
            jax.ShapeDtypeStruct((2, 4, 64, 256), jnp.float32),
            jax.ShapeDtypeStruct((2, 2, 256, pairs), jnp.bfloat16),
        ),
        grid=(2,),
        in_specs=[walkers, walkers, pl.BlockSpec((4, 1, 4, 2, 8, pairs), lambda g: (0, g, 0, 0, 0, 0))],
        out_specs=(
            pl.BlockSpec((1, 4, 64, 256), lambda g: (g, 0, 0, 0)),
            pl.BlockSpec((1, 2, 256, pairs), lambda g: (g, 0, 0, 0)),
        ),
        scratch_shapes=[pltpu.VMEM((512, pairs), jnp.bfloat16)],
        compiler_params=pltpu.CompilerParams(vmem_limit_bytes=VMEM_BYTES),
        cost_estimate=pl.CostEstimate(flops=0, bytes_accessed=0, transcendentals=0),
    )(green, green_c, amplitudes.reshape(4, 2, 4, 2, 8, pairs))


def far_terms(green_x, green_xc, rows):
    pairs = green_x.shape[1]
    walkers = pl.BlockSpec((128, pairs), lambda g: (0, 0))
    return pl.pallas_call(
        far_kernel,
        out_shape=jax.ShapeDtypeStruct((2, 4, 64, 256), jnp.float32),
        grid=(2,),
        in_specs=[walkers, walkers, pl.BlockSpec((1, 2, 256, pairs), lambda g: (g, 0, 0, 0))],
        out_specs=pl.BlockSpec((1, 4, 64, 256), lambda g: (g, 0, 0, 0)),
        scratch_shapes=[pltpu.VMEM((512, pairs), jnp.bfloat16)],
        compiler_params=pltpu.CompilerParams(vmem_limit_bytes=20 * 2**20),
        cost_estimate=pl.CostEstimate(flops=0, bytes_accessed=0, transcendentals=0),
    )(green_x, green_xc, rows)


def bias_terms(effective, factors):
    whole = pl.BlockSpec(memory_space=pltpu.VMEM)
    piece = jax.ShapeDtypeStruct((8, 8, 1024), jnp.float32)
    return pl.pallas_call(
        bias_kernel,
        out_shape=(piece, piece),
        in_specs=[whole] * (1 + len(factors)),
        out_specs=(whole, whole),
        compiler_params=pltpu.CompilerParams(vmem_limit_bytes=16 * 2**20),
        cost_estimate=pl.CostEstimate(flops=6 * 32 * 128 * 4096, bytes_accessed=3 * 2**20, transcendentals=0),
    )(effective, *factors)


def by_row_part(terms):
    return jnp.stack([terms[:, :128].reshape(2, 32, 128), terms[:, 128:].reshape(2, 32, 128)], axis=1)


def per_device(green, amplitudes, cholesky):
    green_x = move(green, "xh")
    green_c = move(green, "c")
    others = [from_above(cholesky, "zh", k) for k in (1, 2, 3)]

    near, rows = near_terms(green, green_c, amplitudes)
    near = exchange(near.reshape(8, 64, 256), ("z0", "y"))
    owned = jnp.concatenate([cholesky] + others)
    up, down = from_above(owned, "y", 1), from_above(owned, "y", 3)
    near, green_x, owned = lax.optimization_barrier((near, green_x, owned))
    far = far_terms(green_x, move(green_x, "c"), rows)
    far, up = lax.optimization_barrier((far, up))
    far = exchange(far.reshape(8, 64, 256), ("z0", "y"))
    far, up, down = lax.optimization_barrier((far, up, down))
    left, right = from_above(up[:, :2048], "y", 1), from_above(down[:, 2048:], "y", 3)
    factors = [owned, up, left, right, down]

    near, far = by_row_part(jnp.sum(near, axis=0)), by_row_part(jnp.sum(far, axis=0))
    blocks = jnp.concatenate([near, far])
    blocks = jnp.where(lax.axis_index("xh") == 1, jnp.concatenate([far, near]), blocks)
    swapped = jnp.stack([blocks[1], blocks[0], blocks[3], blocks[2]])
    blocks = jnp.where(lax.axis_index("c") == 1, swapped, blocks)
    effective = exchange(blocks.reshape(8, 32, 128), ("zh", "xl"))

    mine, theirs = bias_terms(effective, factors)
    bias = exchange(mine + move(theirs, "c"), ("xh", "z0", "xl"))
    return jnp.sum(bias, axis=0)


def solution(mesh):
    parts = Mesh(mesh.devices.reshape(tuple(SIZES.values())), AXES)
    return jax.shard_map(
        per_device,
        mesh=parts,
        in_specs=(P(ROW, COL), P(ROW, COL), P(AXES, None)),
        out_specs=P(COL, ROW),
        check_vma=False,
    )
```
